512 devices in a mesh: wide: 64 (over y, z), narrow: 8 (over x, core).
Axes of the slice: x: 4, y: 8, z: 8, core: 2. Of those that a mesh axis runs over, the one named last changes fastest.
Arguments:
- noise: bfloat16 [1024, 81920], P('narrow', 'wide'), may hold values from -6 to 6
- latents: bfloat16 [3072, 81920], P('narrow', 'wide'), may hold values from -18 to 18
Outputs:
- velocity: bfloat16 [1024, 81920], P('narrow', 'wide')
The draws below stay inside these ranges and needn't reach their ends.
All inputs are finite; a program needn't handle non-finite values.
Results may differ from the reference program's by a relative error of at most 0.009.
Values may be sent and summed in bfloat16 or wider, within the bound.
No kernel may reach another device: no remote copies, remote signals or barrier semaphores. Data moves between devices by JAX's collectives and lax.ppermute only.
A program may use at most 64 MiB of HBM per device.

```python
import math
import jax
import jax.numpy as jnp
from jax import lax

F = 81920
LD = 384
BALANCE_ROUNDS = 3
NOISE = 1024
LAT = 3072
N_NARROW = 8


def draw_noise(key, part):
    key = jax.random.fold_in(key, 11)
    values = jnp.clip(jax.random.normal(key, (NOISE, F), jnp.float32), -6.0, 6.0)
    return values.astype(jnp.bfloat16)


def draw_latents(key, part):
    key = jax.random.fold_in(key, 23)
    key_values, key_scales = jax.random.split(key)
    scales = jnp.exp(jax.random.uniform(key_scales, (LAT, 1), jnp.float32, -1.2039728, 1.0986123))
    values = jnp.clip(jax.random.normal(key_values, (LAT, F), jnp.float32), -6.0, 6.0)
    return (values * scales).astype(jnp.bfloat16)


def setup_inputs(seed: int = 0) -> dict:
    seeds = jax.random.split(jax.random.key(seed), 3)
    return {
        "noise": draw_noise(jax.random.fold_in(seeds[2], 71), 0),
        "latents": draw_latents(jax.random.fold_in(seeds[2], 71), 0),
    }


def reference(noise, latents):
    inv_root = 1.0 / math.sqrt(F)
    affinity_scores = jnp.dot(noise, latents.T, preferred_element_type=jnp.float32) * inv_root
    kernel = jnp.exp(affinity_scores)
    col_scale = jnp.ones((LAT,), jnp.float32)
    for iteration_step in range(BALANCE_ROUNDS):
        row_total = jnp.dot(kernel, col_scale, precision=lax.Precision.HIGHEST)
        row_scale = 1.0 / NOISE / row_total
        column_mass_total = jnp.dot(kernel.T, row_scale, precision=lax.Precision.HIGHEST)
        col_scale = 1.0 / LAT / column_mass_total
    final_total = jnp.dot(kernel, col_scale, precision=lax.Precision.HIGHEST)
    weights = (kernel * col_scale[None, :] / final_total[:, None]).astype(jnp.bfloat16)
    target = jnp.zeros((NOISE, F), jnp.float32)
    for index in range(N_NARROW):
        block_weights = weights[:, index * LD:(index + 1) * LD]
        clips_in_block = latents[index * LD:(index + 1) * LD]
        block_target = jnp.dot(block_weights, clips_in_block, preferred_element_type=jnp.float32).astype(jnp.bfloat16)
        target = target + block_target.astype(jnp.float32)
    return (target - noise.astype(jnp.float32)).astype(jnp.bfloat16)
```

```python
import math

import jax
import jax.numpy as jnp
from jax import lax
from jax.sharding import PartitionSpec as P

F = 81920
BALANCE_ROUNDS = 3


def narrow_totals(kernel, col_scale):
    return lax.psum(jnp.sum(kernel * col_scale[None, :], axis=1), "narrow")


def body(noise, latents):
    inv_root = 1.0 / math.sqrt(F)
    rows_all = lax.all_gather(noise, "narrow", axis=0, tiled=True)
    total_noise = rows_all.shape[0]
    video_clip_rows = latents.shape[0]
    total_clips = video_clip_rows * lax.axis_size("narrow")
    affinity_scores = lax.psum(jnp.dot(rows_all, latents.T, preferred_element_type=jnp.float32), "wide")
    kernel = jnp.exp(affinity_scores * inv_root)
    col_scale = jnp.ones((video_clip_rows,), jnp.float32)
    for iteration_step in range(BALANCE_ROUNDS):
        row_total = narrow_totals(kernel, col_scale)
        row_scale = 1.0 / total_noise / row_total
        column_mass_total = jnp.sum(kernel * row_scale[:, None], axis=0)
        col_scale = 1.0 / total_clips / column_mass_total
    final_total = narrow_totals(kernel, col_scale)
    weights = (kernel * col_scale[None, :] / final_total[:, None]).astype(jnp.bfloat16)
    partial_value = jnp.dot(weights, latents, preferred_element_type=jnp.float32)
    summed = lax.psum_scatter(
        partial_value.astype(jnp.bfloat16), "narrow", scatter_dimension=0, tiled=True
    ).astype(jnp.float32)
    return (summed - noise.astype(jnp.float32)).astype(jnp.bfloat16)


def solution(mesh):
    in_specs = (P("narrow", "wide"), P("narrow", "wide"))
    out_specs = P("narrow", "wide")
    return jax.shard_map(body, mesh=mesh, in_specs=in_specs, out_specs=out_specs, check_vma=False)
```

```python
import math

import jax
import jax.numpy as jnp
from jax import lax
from jax.sharding import Mesh
from jax.sharding import PartitionSpec as P

F = 81920
BALANCE_ROUNDS = 3
Y, Z, X, C = 8, 8, 4, 2
WIDE = ("y", "z")
NARROW = ("x", "c")
SWAP = [(0, 1), (1, 0)]
SEND_SCALE = 64.0


def gather_by_a2a(block, axes, n):
    return lax.all_to_all(jnp.broadcast_to(block[None], (n, *block.shape)), axes, 0, 0).reshape(
        n * block.shape[0], block.shape[1]
    )


def body(noise, latents):
    draws, features = noise.shape
    clips = latents.shape[0]
    total_noise = draws * X * C
    total_clips = clips * X * C
    half = draws * X
    first_core = lax.axis_index("c") == 0

    own_rows = gather_by_a2a(noise, "x", X)
    other_rows = lax.ppermute(own_rows, "c", SWAP)
    scale = SEND_SCALE / math.sqrt(F)

    def partial_scores(rows):
        scores = lax.dot_general(rows, latents, (((1,), (1,)), ((), ())), preferred_element_type=jnp.float32)
        return (scores * scale).astype(jnp.float16)

    partial = jnp.concatenate([partial_scores(own_rows), partial_scores(other_rows)], axis=0)
    arrived = lax.all_to_all(partial.reshape(Y * Z, total_noise // (Y * Z), clips), WIDE, 0, 0)
    scores = jnp.sum(arrived.astype(jnp.float32), axis=0)
    block = jnp.exp(scores * (1.0 / SEND_SCALE)).astype(jnp.bfloat16)
    kernel = gather_by_a2a(block, WIDE, Y * Z).astype(jnp.float32)

    def swap_order(vector):
        halves = vector.reshape(C, half)
        return jnp.where(first_core, halves, halves[::-1]).reshape(total_noise)

    def narrow_totals(col_scale):
        part = swap_order(jnp.sum(kernel * col_scale[None, :], axis=1))
        parts = lax.all_to_all(jnp.broadcast_to(part.reshape(1, 8, -1), (X * C, 8, total_noise // 8)), NARROW, 0, 0)
        return swap_order(jnp.sum(parts, axis=0).reshape(total_noise))

    col_scale = jnp.ones((clips,), jnp.float32)
    for _ in range(BALANCE_ROUNDS):
        row_scale = 1.0 / total_noise / narrow_totals(col_scale)
        col_scale = 1.0 / total_clips / jnp.sum(kernel * row_scale[:, None], axis=0)
    final_total = narrow_totals(col_scale)
    weights = (kernel * col_scale[None, :] / final_total[:, None]).astype(jnp.bfloat16)

    other_part = jnp.dot(weights[half:], latents, preferred_element_type=jnp.float32).astype(jnp.bfloat16)
    from_other = lax.ppermute(other_part, "c", SWAP)
    own_part = jnp.dot(weights[:half], latents, preferred_element_type=jnp.float32)
    pair = (own_part + from_other.astype(jnp.float32)).astype(jnp.bfloat16)
    parts = lax.all_to_all(pair.reshape(X, draws, features), "x", 0, 0)
    target = jnp.sum(parts.astype(jnp.float32), axis=0)
    return (target - noise.astype(jnp.float32)).astype(jnp.bfloat16)


def solution(mesh):
    mesh = Mesh(mesh.devices.reshape(Y, Z, X, C), (*WIDE, *NARROW))
    spec = P(NARROW, WIDE)
    return jax.shard_map(body, mesh=mesh, in_specs=(spec, spec), out_specs=spec, check_vma=False)
```

```python
import math

import jax
import jax.numpy as jnp
from jax import lax
from jax.sharding import Mesh
from jax.sharding import PartitionSpec as P

F = 81920
BALANCE_ROUNDS = 3
Y, Z, X, C = 8, 8, 4, 2
WIDE = ("y", "z")
NARROW = ("x", "c")
SWAP = [(0, 1), (1, 0)]
SEND_SCALE = 64.0


def gather_by_a2a(block, axes, n):
    return lax.all_to_all(jnp.broadcast_to(block[None], (n, *block.shape)), axes, 0, 0).reshape(
        n * block.shape[0], block.shape[1]
    )


def body(noise, latents):
    draws, features = noise.shape
    total_noise = draws * X * C
    total_clips = latents.shape[0] * X * C
    rows = draws * X
    clips = latents.shape[0] * C

    other = lax.ppermute(latents, "c", SWAP)
    chip_latents = jnp.where(
        lax.axis_index("c") == 0,
        jnp.concatenate([latents, other], axis=0),
        jnp.concatenate([other, latents], axis=0),
    )
    noise_rows = gather_by_a2a(noise, "x", X)
    scores = lax.dot_general(noise_rows, chip_latents, (((1,), (1,)), ((), ())), preferred_element_type=jnp.float32)
    partial = (scores * (SEND_SCALE / math.sqrt(F))).astype(jnp.float16)
    arrived = lax.all_to_all(partial.reshape(Y * Z, rows // (Y * Z), clips), WIDE, 0, 0)
    block = jnp.exp(jnp.sum(arrived.astype(jnp.float32), axis=0) * (1.0 / SEND_SCALE))
    kernel = gather_by_a2a(block.astype(jnp.bfloat16), WIDE, Y * Z).astype(jnp.float32)

    col_scale = jnp.ones((clips,), jnp.float32)
    for _ in range(BALANCE_ROUNDS):
        part = jnp.sum(kernel * col_scale[None, :], axis=1).reshape(1, rows // 128, 128)
        parts = lax.all_to_all(jnp.broadcast_to(part, (X, *part.shape[1:])), "x", 0, 0)
        row_scale = 1.0 / total_noise / jnp.sum(parts, axis=0).reshape(rows)
        col_scale = 1.0 / total_clips / lax.psum(jnp.sum(kernel * row_scale[:, None], axis=0), "c")

    plan = kernel * col_scale[None, :] * (row_scale * total_noise)[:, None]
    partial_target = jnp.dot(plan.astype(jnp.bfloat16), chip_latents, preferred_element_type=jnp.float32)
    parts = lax.all_to_all(partial_target.astype(jnp.bfloat16).reshape(X, draws, features), "x", 0, 0)
    final_total = lax.psum(jnp.sum(plan, axis=1).reshape(X, draws), "x")
    own_total = lax.dynamic_index_in_dim(final_total, lax.axis_index("x"), 0, keepdims=False)
    target = jnp.sum(parts.astype(jnp.float32), axis=0) / own_total[:, None]
    return (target - noise.astype(jnp.float32)).astype(jnp.bfloat16)


def solution(mesh):
    mesh = Mesh(mesh.devices.reshape(Y, Z, X, C), (*WIDE, *NARROW))
    spec = P(NARROW, WIDE)
    return jax.shard_map(body, mesh=mesh, in_specs=(spec, spec), out_specs=spec, check_vma=False)
```

```python
import math

import jax
import jax.numpy as jnp
from jax import lax
from jax.sharding import Mesh
from jax.sharding import PartitionSpec as P

F = 81920
BALANCE_ROUNDS = 3
Y, Z, X, C = 8, 8, 4, 2
WIDE = ("y", "z")
NARROW = ("x", "c")
SWAP = [(0, 1), (1, 0)]
SEND_SCALE = 64.0
LANES = 128
TILE = 8


def gather_by_a2a(block, axes, n):
    return lax.all_to_all(jnp.broadcast_to(block[None], (n, *block.shape)), axes, 0, 0).reshape(
        n * block.shape[0], block.shape[1]
    )


def sum_over_x(*parts):
    sizes = [p.shape[0] // LANES for p in parts]
    send = jnp.concatenate([p.reshape(1, -1, LANES) for p in parts], axis=1)
    total = jnp.sum(lax.all_to_all(jnp.broadcast_to(send, (X, *send.shape[1:])), "x", 0, 0), axis=0)
    out, at = [], 0
    for size in sizes:
        out.append(total[at : at + size].reshape(size * LANES))
        at += size
    return out


def body(noise, latents):
    draws, features = noise.shape
    total_noise = draws * X * C
    total_clips = latents.shape[0] * X * C
    rows = draws * X
    clips = latents.shape[0] * C

    other = lax.ppermute(latents, "c", SWAP)
    chip_latents = jnp.where(
        lax.axis_index("c") == 0,
        jnp.concatenate([latents, other], axis=0),
        jnp.concatenate([other, latents], axis=0),
    )
    noise_rows = gather_by_a2a(noise, "x", X)
    scores = lax.dot_general(noise_rows, chip_latents, (((1,), (1,)), ((), ())), preferred_element_type=jnp.float32)
    partial = (scores * (SEND_SCALE / math.sqrt(F))).astype(jnp.float16)
    arrived = lax.all_to_all(partial.reshape(Y * Z, rows // (Y * Z), clips), WIDE, 0, 0)
    block = jnp.exp(jnp.sum(arrived.astype(jnp.float32), axis=0) * (1.0 / SEND_SCALE))
    own = gather_by_a2a(block.astype(jnp.bfloat16), WIDE, Y * Z)
    halves = [own, lax.ppermute(own, "c", SWAP)]

    def row_part(kernel, col_scale):
        return jnp.sum(kernel.astype(jnp.float32) * col_scale[None, :], axis=1)

    def col_part(kernel, row_scale):
        return jnp.sum(kernel.astype(jnp.float32) * row_scale[:, None], axis=0)

    (row_total,) = sum_over_x(jnp.sum(own.astype(jnp.float32), axis=1))
    row_scale = 1.0 / total_noise / row_total
    col_scale = 1.0 / total_clips / lax.psum(col_part(own, row_scale), "c")
    for _ in range(BALANCE_ROUNDS - 1):
        row_scales = [1.0 / total_noise / t for t in sum_over_x(*(row_part(k, col_scale) for k in halves))]
        row_scale = row_scales[0]
        col_scale = 1.0 / total_clips / (col_part(halves[0], row_scales[0]) + col_part(halves[1], row_scales[1]))

    plan = own.astype(jnp.float32) * col_scale[None, :] * (row_scale * total_noise)[:, None]
    weights = lax.optimization_barrier(plan.astype(jnp.bfloat16))
    last = jnp.sum(plan, axis=1).reshape(X, 1, draws)
    high = lax.reduce_precision(last, 8, 7)
    totals = jnp.concatenate([high, last - high], axis=1).astype(jnp.bfloat16)
    totals = jnp.pad(totals, ((0, 0), (0, TILE - 2), (0, features - draws)))
    partial_target = jnp.dot(weights, chip_latents, preferred_element_type=jnp.float32).astype(jnp.bfloat16)
    send = jnp.concatenate([partial_target.reshape(X, draws, features), totals], axis=1)
    parts = jnp.sum(lax.all_to_all(send, "x", 0, 0).astype(jnp.float32), axis=0)
    own_total = parts[draws, :draws] + parts[draws + 1, :draws]
    return (parts[:draws] / own_total[:, None] - noise.astype(jnp.float32)).astype(jnp.bfloat16)


def solution(mesh):
    mesh = Mesh(mesh.devices.reshape(Y, Z, X, C), (*WIDE, *NARROW))
    spec = P(NARROW, WIDE)
    return jax.shard_map(body, mesh=mesh, in_specs=(spec, spec), out_specs=spec, check_vma=False)
```

```python
import math

import jax
import jax.numpy as jnp
from jax import lax
from jax.sharding import Mesh
from jax.sharding import PartitionSpec as P

F = 81920
BALANCE_ROUNDS = 3
Y, Z, X, C = 8, 8, 4, 2
WIDE = ("y", "z")
NARROW = ("x", "c")
SWAP = [(0, 1), (1, 0)]
SEND_SCALE = 64.0
LANES = 128
TILE = 8


def gather_by_a2a(block, axes, n):
    return lax.all_to_all(jnp.broadcast_to(block[None], (n, *block.shape)), axes, 0, 0)


def sum_over_x(*parts):
    shape = parts[0].shape
    send = jnp.concatenate([p.reshape(1, -1, LANES) for p in parts], axis=1)
    total = jnp.sum(lax.all_to_all(jnp.broadcast_to(send, (X, *send.shape[1:])), "x", 0, 0), axis=0)
    return total.reshape(len(parts), *shape)


def row_part(kernel, col_scale):
    return jnp.sum(kernel.astype(jnp.float32) * col_scale[None, :, None, :], axis=(1, 3))


def col_part(kernel, row_scale):
    return jnp.sum(kernel.astype(jnp.float32) * row_scale[:, None, :, None], axis=(0, 2))


def body(noise, latents):
    draws, features = noise.shape
    block_clips = latents.shape[0]
    total_noise = draws * X * C
    total_clips = block_clips * X * C
    rows = draws * X
    wide = Y * Z
    share = rows // wide

    other = lax.ppermute(latents, "c", SWAP)
    noise_rows = gather_by_a2a(noise, "x", X).reshape(rows, features)

    def partial_scores(block):
        scores = lax.dot_general(noise_rows, block, (((1,), (1,)), ((), ())), preferred_element_type=jnp.float32)
        return (scores * (SEND_SCALE / math.sqrt(F))).astype(jnp.float16).reshape(wide, 1, share, block_clips)

    partial = jnp.concatenate([partial_scores(latents), partial_scores(other)], axis=1)
    arrived = lax.all_to_all(partial, WIDE, 0, 0)
    block = jnp.exp(jnp.sum(arrived.astype(jnp.float32), axis=0) * (1.0 / SEND_SCALE))
    own = gather_by_a2a(block.astype(jnp.bfloat16), WIDE, wide)
    theirs = lax.ppermute(own, "c", SWAP)

    (row_total,) = sum_over_x(jnp.sum(own.astype(jnp.float32), axis=(1, 3)))
    row_scale = 1.0 / total_noise / row_total
    mass = col_part(own, row_scale)
    col_scale = 1.0 / total_clips / (mass + lax.ppermute(mass, "c", SWAP)[::-1])
    for _ in range(BALANCE_ROUNDS - 1):
        row_total, their_total = sum_over_x(row_part(own, col_scale), row_part(theirs, col_scale[::-1]))
        row_scale = 1.0 / total_noise / row_total
        mass = col_part(own, row_scale) + col_part(theirs, 1.0 / total_noise / their_total)[::-1]
        col_scale = 1.0 / total_clips / mass

    plan = own.astype(jnp.float32) * col_scale[None, :, None, :] * (row_scale * total_noise)[:, None, :, None]
    own_w, other_w = (plan[:, b].reshape(rows, block_clips).astype(jnp.bfloat16) for b in range(C))
    own_w, other_w = lax.optimization_barrier((own_w, other_w))
    last = jnp.sum(plan, axis=(1, 3)).reshape(X, 1, draws)
    high = lax.reduce_precision(last, 8, 7)
    totals = jnp.concatenate([high, last - high], axis=1).astype(jnp.bfloat16)
    totals = jnp.pad(totals, ((0, 0), (0, TILE - 2), (0, features - draws)))
    partial_target = jnp.dot(own_w, latents, preferred_element_type=jnp.float32)
    partial_target += jnp.dot(other_w, other, preferred_element_type=jnp.float32)
    send = jnp.concatenate([partial_target.astype(jnp.bfloat16).reshape(X, draws, features), totals], axis=1)
    parts = jnp.sum(lax.all_to_all(send, "x", 0, 0).astype(jnp.float32), axis=0)
    own_total = parts[draws, :draws] + parts[draws + 1, :draws]
    return (parts[:draws] / own_total[:, None] - noise.astype(jnp.float32)).astype(jnp.bfloat16)


def solution(mesh):
    mesh = Mesh(mesh.devices.reshape(Y, Z, X, C), (*WIDE, *NARROW))
    spec = P(NARROW, WIDE)
    return jax.shard_map(body, mesh=mesh, in_specs=(spec, spec), out_specs=spec, check_vma=False)
```

```python
import math

import jax
import jax.numpy as jnp
from jax import lax
from jax.sharding import Mesh
from jax.sharding import PartitionSpec as P

F = 81920
BALANCE_ROUNDS = 3
Y, Z, X, C = 8, 8, 4, 2
WIDE = ("y", "z")
NARROW = ("x", "c")
SWAP = [(0, 1), (1, 0)]
SEND_SCALE = 64.0
LANES = 128
TILE = 8


def gather_by_a2a(block, axes, n):
    return lax.all_to_all(jnp.broadcast_to(block[None], (n, *block.shape)), axes, 0, 0)


def sum_over_x(*parts):
    shape = parts[0].shape
    send = jnp.concatenate([p.reshape(1, -1, LANES) for p in parts], axis=1)
    total = jnp.sum(lax.all_to_all(jnp.broadcast_to(send, (X, *send.shape[1:])), "x", 0, 0), axis=0)
    return total.reshape(len(parts), *shape)


def row_part(kernel, col_scale):
    return jnp.sum(kernel.astype(jnp.float32) * col_scale[None, :, None, :], axis=(1, 3))


def col_part(kernel, row_scale):
    return jnp.sum(kernel.astype(jnp.float32) * row_scale[:, None, :, None], axis=(0, 2))


def body(noise, latents):
    draws, features = noise.shape
    block_clips = latents.shape[0]
    total_noise = draws * X * C
    total_clips = block_clips * X * C
    rows = draws * X
    wide = Y * Z
    share = rows // wide

    other = lax.ppermute(latents, "c", SWAP)
    noise_rows = gather_by_a2a(noise, "x", X).reshape(rows, features)

    def partial_scores(block):
        scores = lax.dot_general(noise_rows, block, (((1,), (1,)), ((), ())), preferred_element_type=jnp.float32)
        return (scores * (SEND_SCALE / math.sqrt(F))).astype(jnp.float16).reshape(wide, 1, share, block_clips)

    partial = jnp.concatenate([partial_scores(latents), partial_scores(other)], axis=1)
    arrived = lax.all_to_all(partial, WIDE, 0, 0)
    block = jnp.exp(jnp.sum(arrived.astype(jnp.float32), axis=0) * (1.0 / SEND_SCALE))
    own = gather_by_a2a(block.astype(jnp.bfloat16), WIDE, wide)
    theirs = lax.ppermute(own, "c", SWAP)

    (row_total,) = sum_over_x(jnp.sum(own.astype(jnp.float32), axis=(1, 3)))
    row_scale = 1.0 / total_noise / row_total
    mass = col_part(own, row_scale)
    col_scale = 1.0 / total_clips / (mass + lax.ppermute(mass, "c", SWAP)[::-1])
    for _ in range(BALANCE_ROUNDS - 1):
        row_total, their_total = sum_over_x(row_part(own, col_scale), row_part(theirs, col_scale[::-1]))
        row_scale = 1.0 / total_noise / row_total
        mass = col_part(own, row_scale) + col_part(theirs, 1.0 / total_noise / their_total)[::-1]
        col_scale = 1.0 / total_clips / mass

    plan = own.astype(jnp.float32) * col_scale[None, :, None, :] * (row_scale * total_noise)[:, None, :, None]
    weights = jnp.concatenate([plan[:, b].reshape(rows, block_clips) for b in range(C)], axis=1)
    weights = lax.optimization_barrier(weights.astype(jnp.bfloat16))
    last = jnp.sum(plan, axis=(1, 3)).reshape(X, 1, draws)
    high = lax.reduce_precision(last, 8, 7)
    totals = jnp.concatenate([high, last - high], axis=1).astype(jnp.bfloat16)
    totals = jnp.pad(totals, ((0, 0), (0, TILE - 2), (0, features - draws)))
    chip_latents = jnp.concatenate([latents, other], axis=0)
    partial_target = jnp.dot(weights, chip_latents, preferred_element_type=jnp.float32)
    send = jnp.concatenate([partial_target.astype(jnp.bfloat16).reshape(X, draws, features), totals], axis=1)
    parts = jnp.sum(lax.all_to_all(send, "x", 0, 0).astype(jnp.float32), axis=0)
    own_total = parts[draws, :draws] + parts[draws + 1, :draws]
    return (parts[:draws] / own_total[:, None] - noise.astype(jnp.float32)).astype(jnp.bfloat16)


def solution(mesh):
    mesh = Mesh(mesh.devices.reshape(Y, Z, X, C), (*WIDE, *NARROW))
    spec = P(NARROW, WIDE)
    return jax.shard_map(body, mesh=mesh, in_specs=(spec, spec), out_specs=spec, check_vma=False)
```

```python
import math

import jax
import jax.numpy as jnp
from jax import lax
from jax.sharding import Mesh
from jax.sharding import PartitionSpec as P

F = 81920
BALANCE_ROUNDS = 3
Y, Z, X, C = 8, 8, 4, 2
WIDE = ("y", "z")
NARROW = ("x", "c")
SWAP = [(0, 1), (1, 0)]
SEND_SCALE = 64.0
LANES = 128
TILE = 8


def gather_by_a2a(block, axes, n):
    return lax.all_to_all(jnp.broadcast_to(block[None], (n, *block.shape)), axes, 0, 0).reshape(
        n * block.shape[0], block.shape[1]
    )


def sum_over_x(*parts):
    sizes = [p.shape[0] // LANES for p in parts]
    send = jnp.concatenate([p.reshape(1, -1, LANES) for p in parts], axis=1)
    got = lax.all_to_all(jnp.broadcast_to(send, (X, *send.shape[1:])), "x", 0, 0)
    total = (got[0] + got[1]) + (got[2] + got[3])
    out, at = [], 0
    for size in sizes:
        out.append(total[at : at + size].reshape(size * LANES))
        at += size
    return out


def body(noise, latents):
    draws, features = noise.shape
    total_noise = draws * X * C
    total_clips = latents.shape[0] * X * C
    rows = draws * X
    clips = latents.shape[0] * C

    other = lax.ppermute(latents, "c", SWAP)
    noise_rows = gather_by_a2a(noise, "x", X)

    def partial_scores(block):
        scores = lax.dot_general(noise_rows, block, (((1,), (1,)), ((), ())), preferred_element_type=jnp.float32)
        return (scores * (SEND_SCALE / math.sqrt(F))).astype(jnp.float16).reshape(Y * Z, 1, rows // (Y * Z), -1)

    partial = jnp.concatenate([partial_scores(latents), partial_scores(other)], axis=1)
    arrived = lax.all_to_all(partial, WIDE, 0, 0)
    scores = jnp.sum(arrived.astype(jnp.float32), axis=0) * (1.0 / SEND_SCALE)
    block = jnp.concatenate([scores[0], scores[1]], axis=1)
    own = lax.optimization_barrier(gather_by_a2a(jnp.exp(block).astype(jnp.bfloat16), WIDE, Y * Z))
    theirs = lax.ppermute(own, "c", SWAP)

    def flip(vector):
        return jnp.roll(vector, clips // 2)

    def row_part(kernel, col_scale):
        return jnp.sum(kernel.astype(jnp.float32) * col_scale[None, :], axis=1)

    def col_part(kernel, row_scale):
        return jnp.sum(kernel.astype(jnp.float32) * row_scale[:, None], axis=0)

    (row_total,) = sum_over_x(jnp.sum(own.astype(jnp.float32), axis=1))
    row_scale = 1.0 / total_noise / row_total
    mass = col_part(own, row_scale)
    col_scale = 1.0 / total_clips / (mass + flip(lax.ppermute(mass, "c", SWAP)))
    for _ in range(BALANCE_ROUNDS - 1):
        row_total, their_total = sum_over_x(row_part(own, col_scale), row_part(theirs, flip(col_scale)))
        row_scale = 1.0 / total_noise / row_total
        mass = col_part(own, row_scale) + flip(col_part(theirs, 1.0 / total_noise / their_total))
        col_scale = 1.0 / total_clips / mass

    plan = own.astype(jnp.float32) * col_scale[None, :] * (row_scale * total_noise)[:, None]
    weights = lax.optimization_barrier(plan.astype(jnp.bfloat16))
    last = jnp.sum(plan, axis=1).reshape(X, 1, draws)
    high = lax.reduce_precision(last, 8, 7)
    totals = jnp.concatenate([high, last - high], axis=1).astype(jnp.bfloat16)
    totals = jnp.pad(totals, ((0, 0), (0, TILE - 2), (0, features - draws)))
    partial_target = jnp.dot(weights[:, : clips // 2], latents, preferred_element_type=jnp.float32)
    partial_target += jnp.dot(weights[:, clips // 2 :], other, preferred_element_type=jnp.float32)
    send = jnp.concatenate([partial_target.astype(jnp.bfloat16).reshape(X, draws, features), totals], axis=1)
    parts = jnp.sum(lax.all_to_all(send, "x", 0, 0).astype(jnp.float32), axis=0)
    own_total = parts[draws, :draws] + parts[draws + 1, :draws]
    return (parts[:draws] / own_total[:, None] - noise.astype(jnp.float32)).astype(jnp.bfloat16)


def solution(mesh):
    mesh = Mesh(mesh.devices.reshape(Y, Z, X, C), (*WIDE, *NARROW))
    spec = P(NARROW, WIDE)
    return jax.shard_map(body, mesh=mesh, in_specs=(spec, spec), out_specs=spec, check_vma=False)
```

```python
import math

import jax
import jax.numpy as jnp
from jax import lax
from jax.sharding import Mesh
from jax.sharding import PartitionSpec as P

F = 81920
BALANCE_ROUNDS = 3
Y, Z, X, C = 8, 8, 4, 2
WIDE = ("y", "z")
NARROW = ("x", "c")
SWAP = [(0, 1), (1, 0)]
SEND_SCALE = 64.0
LANES = 128
TILE = 8


def gather_by_a2a(block, axes, n):
    return lax.all_to_all(jnp.broadcast_to(block[None], (n, *block.shape)), axes, 0, 0).reshape(
        n * block.shape[0], block.shape[1]
    )


def sum_over_x(*parts):
    sizes = [p.shape[0] // LANES for p in parts]
    send = jnp.concatenate([p.reshape(1, -1, LANES) for p in parts], axis=1)
    got = lax.all_to_all(jnp.broadcast_to(send, (X, *send.shape[1:])), "x", 0, 0)
    total = (got[0] + got[1]) + (got[2] + got[3])
    out, at = [], 0
    for size in sizes:
        out.append(total[at : at + size].reshape(size * LANES))
        at += size
    return out


def body(noise, latents):
    draws, features = noise.shape
    total_noise = draws * X * C
    total_clips = latents.shape[0] * X * C
    rows = draws * X
    clips = latents.shape[0] * C

    other = lax.ppermute(latents, "c", SWAP)
    noise_rows = gather_by_a2a(noise, "x", X)

    def partial_scores(block):
        scores = lax.dot_general(noise_rows, block, (((1,), (1,)), ((), ())), preferred_element_type=jnp.float32)
        return (scores * (SEND_SCALE / math.sqrt(F))).astype(jnp.float16).reshape(Y * Z, 1, rows // (Y * Z), -1)

    partial = jnp.concatenate([partial_scores(latents), partial_scores(other)], axis=1)
    arrived = lax.all_to_all(partial, WIDE, 0, 0)
    scores = jnp.sum(arrived.astype(jnp.float32), axis=0) * (1.0 / SEND_SCALE)
    block = jnp.concatenate([scores[0], scores[1]], axis=1)
    own = lax.optimization_barrier(gather_by_a2a(jnp.exp(block).astype(jnp.bfloat16), WIDE, Y * Z))
    theirs, minus_noise = lax.optimization_barrier((lax.ppermute(own, "c", SWAP), -noise))

    def flip(vector):
        return jnp.roll(vector, clips // 2)

    def row_part(kernel, col_scale):
        return jnp.sum(kernel.astype(jnp.float32) * col_scale[None, :], axis=1)

    def col_part(kernel, row_scale):
        return jnp.sum(kernel.astype(jnp.float32) * row_scale[:, None], axis=0)

    col_scale = jnp.ones((clips,), jnp.float32)
    for _ in range(BALANCE_ROUNDS):
        row_total, their_total = sum_over_x(row_part(own, col_scale), row_part(theirs, flip(col_scale)))
        row_scale = 1.0 / total_noise / row_total
        mass = col_part(own, row_scale) + flip(col_part(theirs, 1.0 / total_noise / their_total))
        col_scale = 1.0 / total_clips / mass

    plan = own.astype(jnp.float32) * col_scale[None, :] * (row_scale * total_noise)[:, None]
    weights = lax.optimization_barrier(plan.astype(jnp.bfloat16))
    last = jnp.sum(plan, axis=1).reshape(X, 1, draws)
    high = lax.reduce_precision(last, 8, 7)
    totals = jnp.concatenate([high, last - high], axis=1).astype(jnp.bfloat16)
    totals = jnp.pad(totals, ((0, 0), (0, TILE - 2), (0, features - draws)))
    partial_target = jnp.dot(weights[:, : clips // 2], latents, preferred_element_type=jnp.float32)
    partial_target += jnp.dot(weights[:, clips // 2 :], other, preferred_element_type=jnp.float32)
    send = jnp.concatenate([partial_target.astype(jnp.bfloat16).reshape(X, draws, features), totals], axis=1)
    parts = jnp.sum(lax.all_to_all(send, "x", 0, 0).astype(jnp.float32), axis=0)
    own_total = parts[draws, :draws] + parts[draws + 1, :draws]
    return (parts[:draws] / own_total[:, None] + minus_noise.astype(jnp.float32)).astype(jnp.bfloat16)


def solution(mesh):
    mesh = Mesh(mesh.devices.reshape(Y, Z, X, C), (*WIDE, *NARROW))
    spec = P(NARROW, WIDE)
    return jax.shard_map(body, mesh=mesh, in_specs=(spec, spec), out_specs=spec, check_vma=False)
```

```python
import math

import jax
import jax.numpy as jnp
from jax import lax
from jax.experimental import pallas as pl
from jax.experimental.pallas import tpu as pltpu
from jax.sharding import Mesh
from jax.sharding import PartitionSpec as P

F = 81920
BALANCE_ROUNDS = 3
Y, Z, X, C = 8, 8, 4, 2
WIDE = ("y", "z")
NARROW = ("x", "c")
SWAP = [(0, 1), (1, 0)]
SEND_SCALE = 64.0
LANES = 128
TILE = 8


def gather_by_a2a(block, axes, n):
    return lax.all_to_all(jnp.broadcast_to(block[None], (n, *block.shape)), axes, 0, 0).reshape(
        n * block.shape[0], block.shape[1]
    )


def copy_kernel(block_ref, copies_ref, sems):
    half = block_ref.shape[0] // 2
    copies = []
    for k in range(X):
        for h in range(2):
            part = pl.ds(h * half, half)
            copies.append(pltpu.make_async_copy(block_ref.at[part], copies_ref.at[k, part], sems.at[k, h]))
    for copy in copies:
        copy.start()
    for copy in copies:
        copy.wait()


def copies_for_x(block):
    return pl.pallas_call(
        copy_kernel,
        out_shape=jax.ShapeDtypeStruct((X, *block.shape), block.dtype),
        in_specs=[pl.BlockSpec(memory_space=pltpu.HBM)],
        out_specs=pl.BlockSpec(memory_space=pltpu.HBM),
        scratch_shapes=[pltpu.SemaphoreType.DMA((X, 2))],
        compiler_params=pltpu.CompilerParams(vmem_limit_bytes=4 * 1024 * 1024),
        cost_estimate=pl.CostEstimate(flops=0, bytes_accessed=5 * block.size * 2, transcendentals=0),
        name="noise_copies",
    )(block)


def sum_over_x(*parts):
    sizes = [p.shape[0] // LANES for p in parts]
    send = jnp.concatenate([p.reshape(1, -1, LANES) for p in parts], axis=1)
    got = lax.all_to_all(jnp.broadcast_to(send, (X, *send.shape[1:])), "x", 0, 0)
    total = (got[0] + got[1]) + (got[2] + got[3])
    out, at = [], 0
    for size in sizes:
        out.append(total[at : at + size].reshape(size * LANES))
        at += size
    return out


def body(noise, latents):
    draws, features = noise.shape
    total_noise = draws * X * C
    total_clips = latents.shape[0] * X * C
    rows = draws * X
    clips = latents.shape[0] * C

    other = lax.ppermute(latents, "c", SWAP)
    noise_rows = lax.all_to_all(copies_for_x(noise), "x", 0, 0).reshape(rows, features)

    def partial_scores(block):
        scores = lax.dot_general(noise_rows, block, (((1,), (1,)), ((), ())), preferred_element_type=jnp.float32)
        return (scores * (SEND_SCALE / math.sqrt(F))).astype(jnp.float16).reshape(Y * Z, 1, rows // (Y * Z), -1)

    partial = jnp.concatenate([partial_scores(latents), partial_scores(other)], axis=1)
    arrived = lax.all_to_all(partial, WIDE, 0, 0)
    scores = jnp.sum(arrived.astype(jnp.float32), axis=0) * (1.0 / SEND_SCALE)
    block = jnp.concatenate([scores[0], scores[1]], axis=1)
    own = lax.optimization_barrier(gather_by_a2a(jnp.exp(block).astype(jnp.bfloat16), WIDE, Y * Z))
    theirs, minus_noise = lax.optimization_barrier((lax.ppermute(own, "c", SWAP), -noise))

    def flip(vector):
        return jnp.roll(vector, clips // 2)

    def row_part(kernel, col_scale):
        return jnp.sum(kernel.astype(jnp.float32) * col_scale[None, :], axis=1)

    def col_part(kernel, row_scale):
        return jnp.sum(kernel.astype(jnp.float32) * row_scale[:, None], axis=0)

    col_scale = jnp.ones((clips,), jnp.float32)
    for _ in range(BALANCE_ROUNDS):
        row_total, their_total = sum_over_x(row_part(own, col_scale), row_part(theirs, flip(col_scale)))
        row_scale = 1.0 / total_noise / row_total
        mass = col_part(own, row_scale) + flip(col_part(theirs, 1.0 / total_noise / their_total))
        col_scale = 1.0 / total_clips / mass

    plan = own.astype(jnp.float32) * col_scale[None, :] * (row_scale * total_noise)[:, None]
    weights = lax.optimization_barrier(plan.astype(jnp.bfloat16))
    last = jnp.sum(plan, axis=1).reshape(X, 1, draws)
    high = lax.reduce_precision(last, 8, 7)
    totals = jnp.concatenate([high, last - high], axis=1).astype(jnp.bfloat16)
    totals = jnp.pad(totals, ((0, 0), (0, TILE - 2), (0, features - draws)))
    partial_target = jnp.dot(weights[:, : clips // 2], latents, preferred_element_type=jnp.float32)
    partial_target += jnp.dot(weights[:, clips // 2 :], other, preferred_element_type=jnp.float32)
    send = jnp.concatenate([partial_target.astype(jnp.bfloat16).reshape(X, draws, features), totals], axis=1)
    parts = jnp.sum(lax.all_to_all(send, "x", 0, 0).astype(jnp.float32), axis=0)
    own_total = parts[draws, :draws] + parts[draws + 1, :draws]
    return (parts[:draws] / own_total[:, None] + minus_noise.astype(jnp.float32)).astype(jnp.bfloat16)


def solution(mesh):
    mesh = Mesh(mesh.devices.reshape(Y, Z, X, C), (*WIDE, *NARROW))
    spec = P(NARROW, WIDE)
    return jax.shard_map(body, mesh=mesh, in_specs=(spec, spec), out_specs=spec, check_vma=False)
```

```python
import math

import jax
import jax.numpy as jnp
from jax import lax
from jax.experimental import pallas as pl
from jax.experimental.pallas import tpu as pltpu
from jax.sharding import Mesh
from jax.sharding import PartitionSpec as P

F = 81920
BALANCE_ROUNDS = 3
Y, Z, X, C = 8, 8, 4, 2
WIDE = ("y", "z")
NARROW = ("x", "c")
SWAP = [(0, 1), (1, 0)]
SEND_SCALE = 64.0
LANES = 128
TILE = 8


def gather_by_a2a(block, axes, n):
    return lax.all_to_all(jnp.broadcast_to(block[None], (n, *block.shape)), axes, 0, 0).reshape(
        n * block.shape[0], block.shape[1]
    )


def copy_kernel(block_ref, copies_ref, sems):
    half = block_ref.shape[0] // 2
    copies = []
    for k in range(X):
        for h in range(2):
            part = pl.ds(h * half, half)
            copies.append(pltpu.make_async_copy(block_ref.at[part], copies_ref.at[k, part], sems.at[k, h]))
    for copy in copies:
        copy.start()
    for copy in copies:
        copy.wait()


def copies_for_x(block):
    return pl.pallas_call(
        copy_kernel,
        out_shape=jax.ShapeDtypeStruct((X, *block.shape), block.dtype),
        in_specs=[pl.BlockSpec(memory_space=pltpu.HBM)],
        out_specs=pl.BlockSpec(memory_space=pltpu.HBM),
        scratch_shapes=[pltpu.SemaphoreType.DMA((X, 2))],
        compiler_params=pltpu.CompilerParams(vmem_limit_bytes=4 * 1024 * 1024),
        cost_estimate=pl.CostEstimate(flops=0, bytes_accessed=5 * block.size * 2, transcendentals=0),
        name="noise_copies",
    )(pltpu.with_memory_space_constraint(block, pltpu.HBM))


def sum_over_x(*parts):
    sizes = [p.shape[0] // LANES for p in parts]
    send = jnp.concatenate([p.reshape(1, -1, LANES) for p in parts], axis=1)
    got = lax.all_to_all(jnp.broadcast_to(send, (X, *send.shape[1:])), "x", 0, 0)
    total = (got[0] + got[1]) + (got[2] + got[3])
    out, at = [], 0
    for size in sizes:
        out.append(total[at : at + size].reshape(size * LANES))
        at += size
    return out


def body(noise, latents):
    draws, features = noise.shape
    total_noise = draws * X * C
    total_clips = latents.shape[0] * X * C
    rows = draws * X
    clips = latents.shape[0] * C

    other = lax.ppermute(latents, "c", SWAP)
    noise_rows = lax.all_to_all(copies_for_x(noise), "x", 0, 0).reshape(rows, features)

    def partial_scores(block):
        scores = lax.dot_general(noise_rows, block, (((1,), (1,)), ((), ())), preferred_element_type=jnp.float32)
        return (scores * (SEND_SCALE / math.sqrt(F))).astype(jnp.float16).reshape(Y * Z, 1, rows // (Y * Z), -1)

    partial = jnp.concatenate([partial_scores(latents), partial_scores(other)], axis=1)
    arrived = lax.all_to_all(partial, WIDE, 0, 0)
    scores = jnp.sum(arrived.astype(jnp.float32), axis=0) * (1.0 / SEND_SCALE)
    block = jnp.concatenate([scores[0], scores[1]], axis=1)
    own = lax.optimization_barrier(gather_by_a2a(jnp.exp(block).astype(jnp.bfloat16), WIDE, Y * Z))
    theirs, minus_noise = lax.optimization_barrier((lax.ppermute(own, "c", SWAP), -noise))

    def flip(vector):
        return jnp.roll(vector, clips // 2)

    def row_part(kernel, col_scale):
        return jnp.sum(kernel.astype(jnp.float32) * col_scale[None, :], axis=1)

    def col_part(kernel, row_scale):
        return jnp.sum(kernel.astype(jnp.float32) * row_scale[:, None], axis=0)

    col_scale = jnp.ones((clips,), jnp.float32)
    for _ in range(BALANCE_ROUNDS):
        row_total, their_total = sum_over_x(row_part(own, col_scale), row_part(theirs, flip(col_scale)))
        row_scale = 1.0 / total_noise / row_total
        mass = col_part(own, row_scale) + flip(col_part(theirs, 1.0 / total_noise / their_total))
        col_scale = 1.0 / total_clips / mass

    plan = own.astype(jnp.float32) * col_scale[None, :] * (row_scale * total_noise)[:, None]
    weights = lax.optimization_barrier(plan.astype(jnp.bfloat16))
    last = jnp.sum(plan, axis=1).reshape(X, 1, draws)
    high = lax.reduce_precision(last, 8, 7)
    totals = jnp.concatenate([high, last - high], axis=1).astype(jnp.bfloat16)
    totals = jnp.pad(totals, ((0, 0), (0, TILE - 2), (0, features - draws)))
    partial_target = jnp.dot(weights[:, : clips // 2], latents, preferred_element_type=jnp.float32)
    partial_target += jnp.dot(weights[:, clips // 2 :], other, preferred_element_type=jnp.float32)
    send = jnp.concatenate([partial_target.astype(jnp.bfloat16).reshape(X, draws, features), totals], axis=1)
    parts = jnp.sum(lax.all_to_all(send, "x", 0, 0).astype(jnp.float32), axis=0)
    own_total = parts[draws, :draws] + parts[draws + 1, :draws]
    return (parts[:draws] / own_total[:, None] + minus_noise.astype(jnp.float32)).astype(jnp.bfloat16)


def solution(mesh):
    mesh = Mesh(mesh.devices.reshape(Y, Z, X, C), (*WIDE, *NARROW))
    spec = P(NARROW, WIDE)
    return jax.shard_map(body, mesh=mesh, in_specs=(spec, spec), out_specs=spec, check_vma=False)
```

```python
import math

import jax
import jax.numpy as jnp
from jax import lax
from jax.experimental import pallas as pl
from jax.experimental.pallas import tpu as pltpu
from jax.sharding import Mesh
from jax.sharding import PartitionSpec as P

F = 81920
BALANCE_ROUNDS = 3
Y, Z, X, C = 8, 8, 4, 2
WIDE = ("y", "z")
NARROW = ("x", "c")
SWAP = [(0, 1), (1, 0)]
SEND_SCALE = 64.0
LANES = 128
TILE = 8
PIECES = 4


def gather_by_a2a(block, axes, n):
    return lax.all_to_all(jnp.broadcast_to(block[None], (n, *block.shape)), axes, 0, 0).reshape(
        n * block.shape[0], block.shape[1]
    )


def copy_kernel(block_ref, copies_ref, held, in_sems, out_sems):
    size = block_ref.shape[0] // PIECES
    pieces = [pl.ds(p * size, size) for p in range(PIECES)]
    loads = [pltpu.make_async_copy(block_ref.at[d], held.at[d], in_sems.at[p]) for p, d in enumerate(pieces)]
    for load in loads:
        load.start()
    copies = []
    for p, d in enumerate(pieces):
        loads[p].wait()
        for k in range(X):
            copies.append(pltpu.make_async_copy(held.at[d], copies_ref.at[k, d], out_sems.at[p, k]))
            copies[-1].start()
    for copy in copies:
        copy.wait()


def copies_for_x(block):
    return pl.pallas_call(
        copy_kernel,
        out_shape=jax.ShapeDtypeStruct((X, *block.shape), block.dtype),
        in_specs=[pl.BlockSpec(memory_space=pltpu.HBM)],
        out_specs=pl.BlockSpec(memory_space=pltpu.HBM),
        scratch_shapes=[
            pltpu.VMEM(block.shape, block.dtype),
            pltpu.SemaphoreType.DMA((PIECES,)),
            pltpu.SemaphoreType.DMA((PIECES, X)),
        ],
        compiler_params=pltpu.CompilerParams(vmem_limit_bytes=4 * 1024 * 1024),
        cost_estimate=pl.CostEstimate(flops=0, bytes_accessed=5 * block.size * 2, transcendentals=0),
        name="noise_copies",
    )(pltpu.with_memory_space_constraint(block, pltpu.HBM))


def sum_over_x(*parts):
    sizes = [p.shape[0] // LANES for p in parts]
    send = jnp.concatenate([p.reshape(1, -1, LANES) for p in parts], axis=1)
    got = lax.all_to_all(jnp.broadcast_to(send, (X, *send.shape[1:])), "x", 0, 0)
    total = (got[0] + got[1]) + (got[2] + got[3])
    out, at = [], 0
    for size in sizes:
        out.append(total[at : at + size].reshape(size * LANES))
        at += size
    return out


def body(noise, latents):
    draws, features = noise.shape
    total_noise = draws * X * C
    total_clips = latents.shape[0] * X * C
    rows = draws * X
    clips = latents.shape[0] * C

    other = lax.ppermute(latents, "c", SWAP)
    noise_rows = lax.all_to_all(copies_for_x(noise), "x", 0, 0).reshape(rows, features)

    def partial_scores(block):
        scores = lax.dot_general(noise_rows, block, (((1,), (1,)), ((), ())), preferred_element_type=jnp.float32)
        return (scores * (SEND_SCALE / math.sqrt(F))).astype(jnp.float16).reshape(Y * Z, 1, rows // (Y * Z), -1)

    partial = jnp.concatenate([partial_scores(latents), partial_scores(other)], axis=1)
    arrived = lax.all_to_all(partial, WIDE, 0, 0)
    scores = jnp.sum(arrived.astype(jnp.float32), axis=0) * (1.0 / SEND_SCALE)
    block = jnp.concatenate([scores[0], scores[1]], axis=1)
    own = lax.optimization_barrier(gather_by_a2a(jnp.exp(block).astype(jnp.bfloat16), WIDE, Y * Z))
    theirs, minus_noise = lax.optimization_barrier((lax.ppermute(own, "c", SWAP), -noise))

    def flip(vector):
        return jnp.roll(vector, clips // 2)

    def row_part(kernel, col_scale):
        return jnp.sum(kernel.astype(jnp.float32) * col_scale[None, :], axis=1)

    def col_part(kernel, row_scale):
        return jnp.sum(kernel.astype(jnp.float32) * row_scale[:, None], axis=0)

    col_scale = jnp.ones((clips,), jnp.float32)
    for _ in range(BALANCE_ROUNDS):
        row_total, their_total = sum_over_x(row_part(own, col_scale), row_part(theirs, flip(col_scale)))
        row_scale = 1.0 / total_noise / row_total
        mass = col_part(own, row_scale) + flip(col_part(theirs, 1.0 / total_noise / their_total))
        col_scale = 1.0 / total_clips / mass

    plan = own.astype(jnp.float32) * col_scale[None, :] * (row_scale * total_noise)[:, None]
    weights = lax.optimization_barrier(plan.astype(jnp.bfloat16))
    last = jnp.sum(plan, axis=1).reshape(X, 1, draws)
    high = lax.reduce_precision(last, 8, 7)
    totals = jnp.concatenate([high, last - high], axis=1).astype(jnp.bfloat16)
    totals = jnp.pad(totals, ((0, 0), (0, TILE - 2), (0, features - draws)))
    partial_target = jnp.dot(weights[:, : clips // 2], latents, preferred_element_type=jnp.float32)
    partial_target += jnp.dot(weights[:, clips // 2 :], other, preferred_element_type=jnp.float32)
    send = jnp.concatenate([partial_target.astype(jnp.bfloat16).reshape(X, draws, features), totals], axis=1)
    parts = jnp.sum(lax.all_to_all(send, "x", 0, 0).astype(jnp.float32), axis=0)
    own_total = parts[draws, :draws] + parts[draws + 1, :draws]
    return (parts[:draws] / own_total[:, None] + minus_noise.astype(jnp.float32)).astype(jnp.bfloat16)


def solution(mesh):
    mesh = Mesh(mesh.devices.reshape(Y, Z, X, C), (*WIDE, *NARROW))
    spec = P(NARROW, WIDE)
    return jax.shard_map(body, mesh=mesh, in_specs=(spec, spec), out_specs=spec, check_vma=False)
```

```python
import math

import jax
import jax.numpy as jnp
from jax import lax
from jax.sharding import Mesh
from jax.sharding import PartitionSpec as P

F = 81920
BALANCE_ROUNDS = 3
Y, Z, X, C = 8, 8, 4, 2
NEAR, FAR = ("y_near", "z_near"), ("y_far", "z_far")
WIDE = (*NEAR, *FAR)
NARROW = ("x", "c")
SWAP = [(0, 1), (1, 0)]
SEND_SCALE = 64.0
LANES = 128
TILE = 8


def gather_by_a2a(block, axes, n):
    return lax.all_to_all(jnp.broadcast_to(block[None], (n, *block.shape)), axes, 0, 0).reshape(
        n * block.shape[0], block.shape[1]
    )


def sum_over_x(*parts):
    sizes = [p.shape[0] // LANES for p in parts]
    send = jnp.concatenate([p.reshape(1, -1, LANES) for p in parts], axis=1)
    got = lax.all_to_all(jnp.broadcast_to(send, (X, *send.shape[1:])), "x", 0, 0)
    total = (got[0] + got[1]) + (got[2] + got[3])
    out, at = [], 0
    for size in sizes:
        out.append(total[at : at + size].reshape(size * LANES))
        at += size
    return out


def body(noise, latents):
    draws, features = noise.shape
    total_noise = draws * X * C
    total_clips = latents.shape[0] * X * C
    rows = draws * X
    clips = latents.shape[0] * C

    other = lax.ppermute(latents, "c", SWAP)
    noise_rows = gather_by_a2a(noise, "x", X)

    def partial_scores(block):
        scores = lax.dot_general(noise_rows, block, (((1,), (1,)), ((), ())), preferred_element_type=jnp.float32)
        return (scores * (SEND_SCALE / math.sqrt(F))).astype(jnp.float16).reshape(Y * Z, 1, rows // (Y * Z), -1)

    partial = jnp.concatenate([partial_scores(latents), partial_scores(other)], axis=1)
    arrived = lax.all_to_all(partial, WIDE, 0, 0)
    scores = jnp.sum(arrived.astype(jnp.float32), axis=0) * (1.0 / SEND_SCALE)
    block = jnp.concatenate([scores[0], scores[1]], axis=1)
    own = gather_by_a2a(jnp.exp(block).astype(jnp.bfloat16), FAR, Y * Z // 4)
    own = lax.optimization_barrier(gather_by_a2a(own, NEAR, 4))
    theirs, minus_noise = lax.optimization_barrier((lax.ppermute(own, "c", SWAP), -noise))

    def flip(vector):
        return jnp.roll(vector, clips // 2)

    def row_part(kernel, col_scale):
        return jnp.sum(kernel.astype(jnp.float32) * col_scale[None, :], axis=1)

    def col_part(kernel, row_scale):
        return jnp.sum(kernel.astype(jnp.float32) * row_scale[:, None], axis=0)

    col_scale = jnp.ones((clips,), jnp.float32)
    for _ in range(BALANCE_ROUNDS):
        row_total, their_total = sum_over_x(row_part(own, col_scale), row_part(theirs, flip(col_scale)))
        row_scale = 1.0 / total_noise / row_total
        mass = col_part(own, row_scale) + flip(col_part(theirs, 1.0 / total_noise / their_total))
        col_scale = 1.0 / total_clips / mass

    plan = own.astype(jnp.float32) * col_scale[None, :] * (row_scale * total_noise)[:, None]
    weights = lax.optimization_barrier(plan.astype(jnp.bfloat16))
    last = jnp.sum(plan, axis=1).reshape(X, 1, draws)
    high = lax.reduce_precision(last, 8, 7)
    totals = jnp.concatenate([high, last - high], axis=1).astype(jnp.bfloat16)
    totals = jnp.pad(totals, ((0, 0), (0, TILE - 2), (0, features - draws)))
    partial_target = jnp.dot(weights[:, : clips // 2], latents, preferred_element_type=jnp.float32)
    partial_target += jnp.dot(weights[:, clips // 2 :], other, preferred_element_type=jnp.float32)
    send = jnp.concatenate([partial_target.astype(jnp.bfloat16).reshape(X, draws, features), totals], axis=1)
    parts = jnp.sum(lax.all_to_all(send, "x", 0, 0).astype(jnp.float32), axis=0)
    own_total = parts[draws, :draws] + parts[draws + 1, :draws]
    return (parts[:draws] / own_total[:, None] + minus_noise.astype(jnp.float32)).astype(jnp.bfloat16)


def solution(mesh):
    axes = ("y_far", "y_near", "z_far", "z_near")
    mesh = Mesh(mesh.devices.reshape(Y // 2, 2, Z // 2, 2, X, C), (*axes, *NARROW))
    spec = P(NARROW, axes)
    return jax.shard_map(body, mesh=mesh, in_specs=(spec, spec), out_specs=spec, check_vma=False)
```

```python
import math

import jax
import jax.numpy as jnp
from jax import lax
from jax.sharding import Mesh
from jax.sharding import PartitionSpec as P

F = 81920
BALANCE_ROUNDS = 3
Y, Z, X, C = 8, 8, 4, 2
NEAR, FAR = ("y_near", "z_near"), ("y_far", "z_far")
WIDE = ("y_far", "y_near", "z_far", "z_near")
NARROW = ("x", "c")
SWAP = [(0, 1), (1, 0)]
SEND_SCALE = 64.0
LANES = 128
TILE = 8


def gather_by_a2a(block, axes, n):
    return lax.all_to_all(jnp.broadcast_to(block[None], (n, *block.shape)), axes, 0, 0).reshape(
        n * block.shape[0], block.shape[1]
    )


def sum_over_x(*parts):
    sizes = [p.shape[0] // LANES for p in parts]
    send = jnp.concatenate([p.reshape(1, -1, LANES) for p in parts], axis=1)
    got = lax.all_to_all(jnp.broadcast_to(send, (X, *send.shape[1:])), "x", 0, 0)
    total = (got[0] + got[1]) + (got[2] + got[3])
    out, at = [], 0
    for size in sizes:
        out.append(total[at : at + size].reshape(size * LANES))
        at += size
    return out


def body(noise, latents):
    draws, features = noise.shape
    total_noise = draws * X * C
    total_clips = latents.shape[0] * X * C
    rows = draws * X
    clips = latents.shape[0] * C

    other = lax.ppermute(latents, "c", SWAP)
    noise_rows = gather_by_a2a(noise, "x", X)

    def partial_scores(block):
        scores = lax.dot_general(noise_rows, block, (((1,), (1,)), ((), ())), preferred_element_type=jnp.float32)
        return (scores * (SEND_SCALE / math.sqrt(F))).astype(jnp.float16).reshape(Y * Z, 1, rows // (Y * Z), -1)

    partial = jnp.concatenate([partial_scores(latents), partial_scores(other)], axis=1)
    shape = partial.shape
    partial = partial.reshape(2, 2, Y // 2, Z // 2, *shape[1:]).transpose(2, 0, 3, 1, 4, 5, 6).reshape(shape)
    arrived = lax.all_to_all(partial, WIDE, 0, 0)
    scores = jnp.sum(arrived.astype(jnp.float32), axis=0) * (1.0 / SEND_SCALE)
    block = jnp.concatenate([scores[0], scores[1]], axis=1)
    own = gather_by_a2a(jnp.exp(block).astype(jnp.bfloat16), FAR, Y * Z // 4)
    own = lax.optimization_barrier(gather_by_a2a(own, NEAR, 4))
    theirs, minus_noise = lax.optimization_barrier((lax.ppermute(own, "c", SWAP), -noise))

    def flip(vector):
        return jnp.roll(vector, clips // 2)

    def row_part(kernel, col_scale):
        return jnp.sum(kernel.astype(jnp.float32) * col_scale[None, :], axis=1)

    def col_part(kernel, row_scale):
        return jnp.sum(kernel.astype(jnp.float32) * row_scale[:, None], axis=0)

    col_scale = jnp.ones((clips,), jnp.float32)
    for _ in range(BALANCE_ROUNDS):
        row_total, their_total = sum_over_x(row_part(own, col_scale), row_part(theirs, flip(col_scale)))
        row_scale = 1.0 / total_noise / row_total
        mass = col_part(own, row_scale) + flip(col_part(theirs, 1.0 / total_noise / their_total))
        col_scale = 1.0 / total_clips / mass

    plan = own.astype(jnp.float32) * col_scale[None, :] * (row_scale * total_noise)[:, None]
    weights = lax.optimization_barrier(plan.astype(jnp.bfloat16))
    last = jnp.sum(plan, axis=1).reshape(X, 1, draws)
    high = lax.reduce_precision(last, 8, 7)
    totals = jnp.concatenate([high, last - high], axis=1).astype(jnp.bfloat16)
    totals = jnp.pad(totals, ((0, 0), (0, TILE - 2), (0, features - draws)))
    partial_target = jnp.dot(weights[:, : clips // 2], latents, preferred_element_type=jnp.float32)
    partial_target += jnp.dot(weights[:, clips // 2 :], other, preferred_element_type=jnp.float32)
    send = jnp.concatenate([partial_target.astype(jnp.bfloat16).reshape(X, draws, features), totals], axis=1)
    parts = jnp.sum(lax.all_to_all(send, "x", 0, 0).astype(jnp.float32), axis=0)
    own_total = parts[draws, :draws] + parts[draws + 1, :draws]
    return (parts[:draws] / own_total[:, None] + minus_noise.astype(jnp.float32)).astype(jnp.bfloat16)


def solution(mesh):
    mesh = Mesh(mesh.devices.reshape(Y // 2, 2, Z // 2, 2, X, C), (*WIDE, *NARROW))
    spec = P(NARROW, WIDE)
    return jax.shard_map(body, mesh=mesh, in_specs=(spec, spec), out_specs=spec, check_vma=False)
```

```python
import math

import jax
import jax.numpy as jnp
from jax import lax
from jax.sharding import Mesh
from jax.sharding import PartitionSpec as P

F = 81920
BALANCE_ROUNDS = 3
Y, Z, X, C = 8, 8, 4, 2
WIDE = ("y", "z")
NARROW = ("x", "c")
SWAP = [(0, 1), (1, 0)]
SEND_SCALE = 64.0
LANES = 128
TILE = 8


def gather_by_a2a(block, axes, n):
    return lax.all_to_all(jnp.broadcast_to(block[None], (n, *block.shape)), axes, 0, 0).reshape(
        n * block.shape[0], block.shape[1]
    )


def sum_over_x(*parts):
    sizes = [p.shape[0] // LANES for p in parts]
    send = jnp.concatenate([p.reshape(1, -1, LANES) for p in parts], axis=1)
    got = lax.all_to_all(jnp.broadcast_to(send, (X, *send.shape[1:])), "x", 0, 0)
    total = (got[0] + got[1]) + (got[2] + got[3])
    out, at = [], 0
    for size in sizes:
        out.append(total[at : at + size].reshape(size * LANES))
        at += size
    return out


def body(noise, latents):
    draws, features = noise.shape
    total_noise = draws * X * C
    total_clips = latents.shape[0] * X * C
    rows = draws * X
    clips = latents.shape[0] * C

    other = lax.ppermute(latents, "c", SWAP)
    noise_rows = gather_by_a2a(noise, "x", X)

    def partial_scores(block):
        scores = lax.dot_general(noise_rows, block, (((1,), (1,)), ((), ())), preferred_element_type=jnp.float32)
        return (scores * (SEND_SCALE / math.sqrt(F))).astype(jnp.float16).reshape(Y * Z, 1, rows // (Y * Z), -1)

    partial = jnp.concatenate([partial_scores(latents), partial_scores(other)], axis=1)
    arrived = lax.all_to_all(partial, WIDE, 0, 0)
    scores = jnp.sum(arrived.astype(jnp.float32), axis=0) * (1.0 / SEND_SCALE)
    block = jnp.concatenate([scores[0], scores[1]], axis=1)
    own = lax.optimization_barrier(gather_by_a2a(jnp.exp(block).astype(jnp.bfloat16), WIDE, Y * Z))
    theirs, minus_noise = lax.optimization_barrier((lax.ppermute(own, "c", SWAP), -noise))

    def flip(vector):
        return jnp.roll(vector, clips // 2)

    def row_part(kernel, col_scale):
        return jnp.sum(kernel.astype(jnp.float32) * col_scale[None, :], axis=1)

    def col_part(kernel, row_scale):
        return jnp.sum(kernel.astype(jnp.float32) * row_scale[:, None], axis=0)

    col_scale = jnp.ones((clips,), jnp.float32)
    for _ in range(BALANCE_ROUNDS):
        row_total, their_total = sum_over_x(row_part(own, col_scale), row_part(theirs, flip(col_scale)))
        row_scale = 1.0 / total_noise / row_total
        mass = col_part(own, row_scale) + flip(col_part(theirs, 1.0 / total_noise / their_total))
        col_scale = 1.0 / total_clips / mass

    plan = own.astype(jnp.float32) * col_scale[None, :] * (row_scale * total_noise)[:, None]
    weights = lax.optimization_barrier(plan.astype(jnp.bfloat16))
    last = jnp.sum(plan, axis=1).reshape(X, 1, draws)
    high = lax.reduce_precision(last, 8, 7)
    totals = jnp.concatenate([high, last - high], axis=1).astype(jnp.bfloat16)
    totals = jnp.pad(totals, ((0, 0), (0, TILE - 2), (0, features - draws)))
    partial_target = jnp.dot(weights[:, : clips // 2], latents, preferred_element_type=jnp.float32)
    partial_target += jnp.dot(weights[:, clips // 2 :], other, preferred_element_type=jnp.float32)
    send = jnp.concatenate([partial_target.astype(jnp.bfloat16).reshape(X, draws, features), totals], axis=1)
    got = lax.all_to_all(send, "x", 0, 0).astype(jnp.float32)
    parts = (got[0, :draws] + got[1, :draws]) + (got[2, :draws] + got[3, :draws])
    own_total = jnp.sum(got[:, draws : draws + 2, :draws], axis=(0, 1))
    return (parts / own_total[:, None] + minus_noise.astype(jnp.float32)).astype(jnp.bfloat16)


def solution(mesh):
    mesh = Mesh(mesh.devices.reshape(Y, Z, X, C), (*WIDE, *NARROW))
    spec = P(NARROW, WIDE)
    return jax.shard_map(body, mesh=mesh, in_specs=(spec, spec), out_specs=spec, check_vma=False)
```

```python
import math

import jax
import jax.numpy as jnp
from jax import lax
from jax.sharding import Mesh
from jax.sharding import PartitionSpec as P

F = 81920
BALANCE_ROUNDS = 3
Y, Z, X, C = 8, 8, 4, 2
WIDE = ("y", "z")
NARROW = ("x", "c")
SWAP = [(0, 1), (1, 0)]
SEND_SCALE = 64.0
LANES = 128
TILE = 8


def gather_by_a2a(block, axes, n):
    return lax.all_to_all(jnp.broadcast_to(block[None], (n, *block.shape)), axes, 0, 0).reshape(
        n * block.shape[0], block.shape[1]
    )


def sum_over_x(*parts):
    sizes = [p.shape[0] // LANES for p in parts]
    send = jnp.concatenate([p.reshape(1, -1, LANES) for p in parts], axis=1)
    got = lax.all_to_all(jnp.broadcast_to(send, (X, *send.shape[1:])), "x", 0, 0)
    total = (got[0] + got[1]) + (got[2] + got[3])
    out, at = [], 0
    for size in sizes:
        out.append(total[at : at + size].reshape(size * LANES))
        at += size
    return out


def body(noise, latents):
    draws, features = noise.shape
    total_noise = draws * X * C
    total_clips = latents.shape[0] * X * C
    rows = draws * X
    clips = latents.shape[0] * C

    other = lax.ppermute(latents, "c", SWAP)
    noise_rows = gather_by_a2a(noise, "x", X)

    def partial_scores(block):
        scores = lax.dot_general(noise_rows, block, (((1,), (1,)), ((), ())), preferred_element_type=jnp.float32)
        return (scores * (SEND_SCALE / math.sqrt(F))).astype(jnp.float16).reshape(Y * Z, 1, rows // (Y * Z), -1)

    partial = jnp.concatenate([partial_scores(latents), partial_scores(other)], axis=1)
    arrived = lax.all_to_all(partial, WIDE, 0, 0)
    scores = jnp.sum(arrived.astype(jnp.float32), axis=0) * (1.0 / SEND_SCALE)
    block = jnp.concatenate([scores[0], scores[1]], axis=1)
    own = lax.optimization_barrier(gather_by_a2a(jnp.exp(block).astype(jnp.bfloat16), WIDE, Y * Z))
    theirs, minus_noise = lax.optimization_barrier((lax.ppermute(own, "c", SWAP), -noise))

    def flip(vector):
        return jnp.roll(vector, clips // 2)

    def row_part(kernel, col_scale):
        return jnp.sum(kernel.astype(jnp.float32) * col_scale[None, :], axis=1)

    def col_part(kernel, row_scale):
        return jnp.sum(kernel.astype(jnp.float32) * row_scale[:, None], axis=0)

    col_scale = jnp.ones((clips,), jnp.float32)
    for _ in range(BALANCE_ROUNDS):
        row_total, their_total = sum_over_x(row_part(own, col_scale), row_part(theirs, flip(col_scale)))
        row_scale = 1.0 / total_noise / row_total
        mass = col_part(own, row_scale) + flip(col_part(theirs, 1.0 / total_noise / their_total))
        col_scale = 1.0 / total_clips / mass

    plan = own.astype(jnp.float32) * col_scale[None, :] * (row_scale * total_noise)[:, None]
    weights = lax.optimization_barrier(plan.astype(jnp.bfloat16))
    last = jnp.sum(plan, axis=1).reshape(X, 1, draws)
    high = lax.reduce_precision(last, 8, 7)
    totals = jnp.concatenate([high, last - high], axis=1).astype(jnp.bfloat16)
    totals = jnp.pad(totals, ((0, 0), (0, TILE - 2), (0, features - draws)))
    partial_target = jnp.dot(weights[:, : clips // 2], latents, preferred_element_type=jnp.float32)
    partial_target += jnp.dot(weights[:, clips // 2 :], other, preferred_element_type=jnp.float32)
    send = jnp.concatenate([partial_target.astype(jnp.bfloat16).reshape(X, draws, features), totals], axis=1)
    got = lax.all_to_all(send, "x", 0, 0)
    tail = lax.optimization_barrier(got[:, draws:, :draws])
    own_total = jnp.sum(tail[:, :2].astype(jnp.float32), axis=(0, 1))
    part = [got[k, :draws].astype(jnp.float32) for k in range(X)]
    parts = (part[0] + part[1]) + (part[2] + part[3])
    return (parts / own_total[:, None] + minus_noise.astype(jnp.float32)).astype(jnp.bfloat16)


def solution(mesh):
    mesh = Mesh(mesh.devices.reshape(Y, Z, X, C), (*WIDE, *NARROW))
    spec = P(NARROW, WIDE)
    return jax.shard_map(body, mesh=mesh, in_specs=(spec, spec), out_specs=spec, check_vma=False)
```
